256 devices in a mesh: leaf: 64 (over y, z, core), row: 4 (over x).
Axes of the slice: x: 4, y: 4, z: 8, core: 2. Of those that a mesh axis runs over, the one named last changes fastest.
Arguments:
- fields: bfloat16 [256, 2048, 128], P('leaf', 'row'), may hold values from -6 to 6
- near_blocks: bfloat16 [256, 2048, 2048], P('leaf', 'row'), may hold values from -1 to 1, as said below
- leaf_basis: bfloat16 [256, 2048, 256], P('leaf', 'row'), may hold values from -0.125 to 0.125
- leaf_transfer: bfloat16 [256, 256, 256], P('leaf'), may hold values from -0.3125 to 0.3125
- mid_transfer: bfloat16 [128, 256, 256], P('leaf'), may hold values from -0.3125 to 0.3125
- leaf_couple: bfloat16 [128, 256, 256], P('leaf'), may hold values from -0.375 to 0.375
- mid_couple: bfloat16 [64, 256, 256], P('leaf'), may hold values from -0.375 to 0.375
- cross_transfer: bfloat16 [64, 5, 256, 256], P('leaf'), may hold values from -1 to 1, as said below
- cross_couple: bfloat16 [64, 6, 256, 256], P('leaf'), may hold values from -1 to 1, as said below
Outputs:
- product: bfloat16 [256, 2048, 128], P('leaf', 'row')
The draws below stay inside these ranges and needn't reach their ends.
Inputs may be any that keep to these rules, and one draw needn't show every extreme that they name: Each near_blocks[n] is symmetric. cross_transfer[d, j] is equal for all d with the same d >> j: the transfer matrix of node d >> j at height j + 2. cross_couple[d, j] is equal for all d with the same d >> j, and for siblings it is the transpose of the other's.
All inputs are finite; a program needn't handle non-finite values.
Results may differ from the reference program's by a relative error of at most 0.0038.
Values may be sent and summed in bfloat16 or wider, within the bound.
No kernel may reach another device: no remote copies, remote signals or barrier semaphores. Data moves between devices by JAX's collectives and lax.ppermute only.
A program may use at most 64 MiB of HBM per device.

```python
import jax
import jax.numpy as jnp
from jax import lax

LEAF = 2048
RANK = 256
COLS = 128
XLEV = 6
LEAVES = 256
N_LEAF = 64


def base_normal(key, shape, spread):
    values = jnp.clip(jax.random.normal(key, shape, jnp.float32), -4.0, 4.0)
    return values * spread


def draw_near_blocks(key, part):
    key = jax.random.fold_in(key, 11)

    def one_block(index):
        block_key = jax.random.fold_in(key, index)
        raw = base_normal(block_key, (LEAF, LEAF), 1.0)
        return ((raw + raw.T) / (2.0 * LEAF) ** 0.5).astype(jnp.bfloat16)
    return lax.map(one_block, jnp.arange(LEAVES))


def draw_cross_transfer(key, part):
    key = jax.random.fold_in(key, 12)
    table = base_normal(key, (N_LEAF, XLEV - 1, RANK, RANK), (1.5 * RANK) ** (-0.5))
    heights = jnp.arange(XLEV - 1)
    nodes = jnp.arange(N_LEAF)[:, None] >> heights[None, :]
    return table[nodes, heights[None, :]].astype(jnp.bfloat16)


def draw_cross_couple(key, part):
    key = jax.random.fold_in(key, 13)
    table = base_normal(key, (N_LEAF, XLEV, RANK, RANK), RANK ** (-0.5))
    heights = jnp.arange(XLEV)
    devices = jnp.arange(N_LEAF)[:, None]
    parents = devices >> heights[None, :] + 1
    is_right = devices >> heights[None, :] & 1 == 1
    picked = table[parents, heights[None, :]]
    flipped = jnp.swapaxes(picked, -1, -2)
    return jnp.where(is_right[:, :, None, None], flipped, picked).astype(jnp.bfloat16)


def block_scale(own_key, shape, cuts, low, high):
    loudness = 1.0
    for axis_at, blocks in cuts:
        steps = jax.random.uniform(jax.random.fold_in(jax.random.fold_in(own_key, 6), axis_at), (blocks,), jnp.float32, low / len(cuts), high / len(cuts))
        loudness = loudness * jnp.repeat(jnp.exp(steps), shape[axis_at] // blocks).reshape((-1,) + (1,) * (len(shape) - 1 - axis_at))
    return loudness


def bell_draw(rng, extent, width, most, pieces=(), held_as=jnp.bfloat16):
    result = width * jax.random.normal(rng, extent, jnp.float32)
    if pieces:
        result = result * block_scale(rng, extent, pieces, -0.22, 0.18)
    return jnp.clip(result, -most, most).astype(held_as)


def setup_inputs(seed: int = 0) -> dict:
    key_of = jax.random.split(jax.random.key(seed), 10)
    fields = bell_draw(key_of[0], (LEAVES, LEAF, COLS), 1.0, 6.0, ((0, 64), (1, 4)))
    near_blocks = draw_near_blocks(jax.random.fold_in(key_of[9], 71), 0)
    leaf_basis = bell_draw(key_of[2], (LEAVES, LEAF, RANK), LEAF ** -0.5, 0.125, ((0, 64), (1, 4)))
    leaf_transfer = bell_draw(key_of[3], (LEAVES, RANK, RANK), (RANK + RANK // 2) ** -0.5, 0.3125, ((0, 64),))
    mid_transfer = bell_draw(key_of[4], (LEAVES // 2, RANK, RANK), (RANK + RANK // 2) ** -0.5, 0.3125, ((0, 64),))
    leaf_couple = bell_draw(key_of[5], (LEAVES // 2, RANK, RANK), RANK ** -0.5, 0.375, ((0, 64),))
    mid_couple = bell_draw(key_of[6], (LEAVES // 4, RANK, RANK), RANK ** -0.5, 0.375, ((0, 64),))
    cross_transfer = draw_cross_transfer(jax.random.fold_in(key_of[9], 71), 0)
    cross_couple = draw_cross_couple(jax.random.fold_in(key_of[9], 71), 0)
    return {"fields": fields, "near_blocks": near_blocks, "leaf_basis": leaf_basis, "leaf_transfer": leaf_transfer, "mid_transfer": mid_transfer, "leaf_couple": leaf_couple, "mid_couple": mid_couple, "cross_transfer": cross_transfer, "cross_couple": cross_couple}


precise = lax.Precision.HIGHEST


def lift(mats, skel):
    return jnp.einsum('nrs,nrc->nsc', mats.astype(jnp.float32), skel, precision=precise)


def push(mats, potential):
    return jnp.einsum('nrs,nsc->nrc', mats.astype(jnp.float32), potential, precision=precise)


def pair_sums(values):
    return values.reshape((-1, 2) + values.shape[1:]).sum(axis=1)


def swap_pairs(values):
    return values.reshape((-1, 2) + values.shape[1:])[:, ::-1].reshape(values.shape)


def couple_pairs(mats, skel):
    mats32 = mats.astype(jnp.float32)
    left_skel = skel[0::2]
    right_skel = skel[1::2]
    to_left = jnp.einsum('prs,psc->prc', mats32, right_skel, precision=precise)
    to_right = jnp.einsum('psr,psc->prc', mats32, left_skel, precision=precise)
    return jnp.stack([to_left, to_right], axis=1).reshape(skel.shape)


def near_one(pair):
    return jnp.dot(pair[0].astype(jnp.float32), pair[1].astype(jnp.float32), precision=precise)


def reference(fields, near_blocks, leaf_basis, leaf_transfer, mid_transfer, leaf_couple, mid_couple, cross_transfer, cross_couple):
    basis32 = leaf_basis.astype(jnp.float32)
    skel_leaf = jnp.einsum('nkr,nkc->nrc', basis32, fields.astype(jnp.float32), precision=precise)
    skel_mid = pair_sums(lift(leaf_transfer, skel_leaf))
    current = pair_sums(lift(mid_transfer, skel_mid))
    stored = [current]
    for height in range(XLEV - 1):
        mats = cross_transfer[::2 ** height, height]
        current = pair_sums(lift(mats, current))
        stored.append(current)
    crown = XLEV - 1
    potential = push(cross_couple[::2 ** crown, crown], swap_pairs(stored[crown]))
    for height in reversed(range(XLEV - 1)):
        mats = cross_transfer[::2 ** height, height]
        couples = cross_couple[::2 ** height, height]
        potential = push(mats, jnp.repeat(potential, 2, axis=0)) + push(couples, swap_pairs(stored[height]))
    pot_mid = push(mid_transfer, jnp.repeat(potential, 2, axis=0)) + couple_pairs(mid_couple, skel_mid)
    pot_leaf = push(leaf_transfer, jnp.repeat(pot_mid, 2, axis=0)) + couple_pairs(leaf_couple, skel_leaf)
    potential_low = pot_leaf.astype(jnp.bfloat16)
    far_part = jnp.einsum('nkr,nrc->nkc', basis32, potential_low.astype(jnp.float32), precision=precise)
    near_part = lax.map(near_one, (near_blocks, fields))
    return (near_part + far_part).astype(jnp.bfloat16)
```

```python
import functools

import jax
import jax.numpy as jnp
from jax import lax
from jax.experimental import pallas as pl
from jax.experimental.pallas import tpu as pltpu
from jax.sharding import PartitionSpec as P

bf16 = jnp.bfloat16
f32 = jnp.float32
precise = lax.Precision.HIGHEST
PARTNERS = (1, 2, 4, 12, 16, 48)


def exchange(value, axis, mask):
    count = lax.axis_size(axis)
    return lax.ppermute(value, axis, [(i, i ^ mask) for i in range(count)])


def shifted(value, step):
    count = lax.axis_size("row")
    return lax.ppermute(value, "row", [(i, (i + step) % count) for i in range(count)])


def times(values, mats):
    return lax.dot_general(
        values, mats.astype(f32), (((1,), (0,)), ((), ())), precision=precise
    )


def times_t(values, mats):
    return lax.dot_general(
        values, mats.astype(f32), (((1,), (1,)), ((), ())), precision=precise
    )


def split_dot(values, mats, contract):
    rows = values.shape[0]
    high = values.astype(bf16)
    low = (values - high.astype(f32)).astype(bf16)
    both = lax.dot_general(
        jnp.concatenate([high, low], axis=0),
        mats,
        (((1,), (contract,)), ((), ())),
        preferred_element_type=f32,
    )
    return both[:rows] + both[rows:]


def after(value, *others):
    return lax.optimization_barrier((value,) + others)[0]


def hold(signal, *values, flops=1 << 24):
    anywhere = pl.BlockSpec(memory_space=pl.ANY)
    return pl.pallas_call(
        lambda *refs: None,
        out_shape=tuple(jax.ShapeDtypeStruct(v.shape, v.dtype) for v in values),
        in_specs=[anywhere] * (1 + len(values)),
        out_specs=(anywhere,) * len(values),
        input_output_aliases={1 + i: i for i in range(len(values))},
        compiler_params=pltpu.CompilerParams(vmem_limit_bytes=16 << 20),
        cost_estimate=pl.CostEstimate(flops=flops, bytes_accessed=0, transcendentals=0),
    )(signal, *values)


def two_terms(values):
    high = lax.reduce_precision(values, 8, 7)
    return high.astype(bf16), (values - high).astype(bf16)


def gather_kernel(
    half,
    fields,
    basis,
    lt,
    mt,
    keep,
    send,
    side_keep,
    side_send,
    f_buf,
    basis_out,
    lt_out,
    mt_out,
    scratch,
    sems,
):
    f_copy = pltpu.make_async_copy(fields, f_buf, sems.at[0])
    b_copies = [
        pltpu.make_async_copy(
            basis.at[pl.ds(2 * pair, 2)], basis_out.at[pl.ds(2 * pair, 2)], sems.at[1 + pair]
        )
        for pair in range(2)
    ]
    lt_copy = pltpu.make_async_copy(lt, lt_out, sems.at[3])
    mt_copy = pltpu.make_async_copy(mt, mt_out, sems.at[4])
    for copy in (f_copy, *b_copies, lt_copy, mt_copy):
        copy.start()
    mine = pl.ds(pl.multiple_of(half[0] * 64, 64), 64)
    other = pl.ds(pl.multiple_of(64 - half[0] * 64, 64), 64)
    f_copy.wait()
    for n in range(4):
        if n % 2 == 0:
            b_copies[n // 2].wait()
        scratch[n] = lax.dot_general(
            f_buf[n], basis_out[n], (((0,), (0,)), ((), ())), preferred_element_type=f32
        )
    lt_copy.wait()
    mt_copy.wait()
    current = None
    for pair in range(2):
        mid = split_dot(scratch[2 * pair], lt_out[2 * pair], 0) + split_dot(
            scratch[2 * pair + 1], lt_out[2 * pair + 1], 0
        )
        lifted = split_dot(mid, mt_out[pair], 0)
        current = lifted if current is None else current + lifted
    scratch[4] = current
    keep[...] = scratch[4, mine, :]
    send[...] = scratch[4, other, :]
    for n in range(4):
        side_keep[n] = scratch[n, mine, :]
        side_send[n] = scratch[n, other, :].astype(bf16)


def gather_skeletons(half, fields, basis, lt, mt):
    vmem = pl.BlockSpec(memory_space=pltpu.VMEM)
    return pl.pallas_call(
        gather_kernel,
        out_shape=(
            jax.ShapeDtypeStruct((64, 256), f32),
            jax.ShapeDtypeStruct((64, 256), f32),
            jax.ShapeDtypeStruct((4, 64, 256), f32),
            jax.ShapeDtypeStruct((4, 64, 256), bf16),
        ),
        in_specs=[pl.BlockSpec(memory_space=pltpu.SMEM)] + [pl.BlockSpec(memory_space=pl.ANY)] * 4,
        out_specs=(vmem,) * 4,
        scratch_shapes=[
            pltpu.VMEM((4, 512, 128), bf16),
            pltpu.VMEM((4, 512, 256), bf16),
            pltpu.VMEM((4, 256, 256), bf16),
            pltpu.VMEM((2, 256, 256), bf16),
            pltpu.VMEM((5, 128, 256), f32),
            pltpu.SemaphoreType.DMA((5,)),
        ],
        compiler_params=pltpu.CompilerParams(vmem_limit_bytes=54528 << 10),
        cost_estimate=pl.CostEstimate(
            flops=2 * 4 * 512 * 256 * 128, bytes_accessed=3 << 20, transcendentals=0
        ),
    )(half, fields, basis, lt, mt)


def stage_kernel(keep, ct, cc, lc, mc, joint, crown, lc_out, mc_out, sems):
    copies = [
        pltpu.make_async_copy(ct.at[0], joint.at[:, :, pl.ds(0, 256)], sems.at[0]),
        pltpu.make_async_copy(
            cc.at[0, pl.ds(0, 5)], joint.at[:, :, pl.ds(256, 256)], sems.at[1]
        ),
        pltpu.make_async_copy(cc.at[0, 5], crown, sems.at[2]),
        pltpu.make_async_copy(lc, lc_out, sems.at[3]),
        pltpu.make_async_copy(mc, mc_out, sems.at[4]),
    ]
    for copy in copies:
        copy.start()
    for copy in copies:
        copy.wait()


def stage_mats(keep, ct, cc, lc, mc):
    vmem = pl.BlockSpec(memory_space=pltpu.VMEM)
    return pl.pallas_call(
        stage_kernel,
        out_shape=(
            jax.ShapeDtypeStruct((5, 256, 512), bf16),
            jax.ShapeDtypeStruct((256, 256), bf16),
            jax.ShapeDtypeStruct((2, 256, 256), bf16),
            jax.ShapeDtypeStruct((1, 256, 256), bf16),
        ),
        in_specs=[pl.BlockSpec(memory_space=pl.ANY)] * 5,
        out_specs=(vmem,) * 4,
        scratch_shapes=[pltpu.SemaphoreType.DMA((5,))],
        compiler_params=pltpu.CompilerParams(vmem_limit_bytes=16 << 20),
        cost_estimate=pl.CostEstimate(flops=0, bytes_accessed=4 << 20, transcendentals=0),
    )(keep, ct, cc, lc, mc)


def near_kernel(offsets, pieces, started, place, near, signal, *refs):
    parts, refs = refs[:pieces], refs[pieces:]
    out = refs[-1]
    for n in range(4):
        total = refs[0][n] if started else None
        for i, offset in enumerate(offsets):
            column = pl.multiple_of(lax.rem(place[0] + offset, 4) * 512, 512)
            part = parts[i][n] if len(offsets) == pieces else parts[n // 2][n % 2]
            term = jnp.dot(near[n, :, pl.ds(column, 512)], part, preferred_element_type=f32)
            total = term if total is None else total + term
        out[n] = total


def near_product(place, near, signal, offsets, parts, so_far=None):
    vmem = pl.BlockSpec(memory_space=pltpu.VMEM)
    extra = () if so_far is None else (so_far,)
    return pl.pallas_call(
        functools.partial(near_kernel, offsets, len(parts), bool(extra)),
        out_shape=jax.ShapeDtypeStruct((4, 512, 128), f32),
        in_specs=[pl.BlockSpec(memory_space=pltpu.SMEM), vmem, pl.BlockSpec(memory_space=pl.ANY)]
        + [vmem] * (len(parts) + len(extra)),
        out_specs=vmem,
        compiler_params=pltpu.CompilerParams(vmem_limit_bytes=24 << 20),
        cost_estimate=pl.CostEstimate(
            flops=1 << 31, bytes_accessed=1 << 12, transcendentals=0
        ),
    )(place, near, signal, *parts, *extra)


def side_kernel(signal, own, got, lt, lc, mc, out, out_low, skel):
    for n in range(4):
        skel[n] = own[n] + got[n].astype(f32)
    mid = [
        split_dot(skel[2 * pair], lt[2 * pair], 0)
        + split_dot(skel[2 * pair + 1], lt[2 * pair + 1], 0)
        for pair in range(2)
    ]
    for pair in range(2):
        pot_mid = split_dot(mid[1 - pair], mc[0], 1 - pair)
        for k in range(2):
            n = 2 * pair + k
            out[n] = split_dot(skel[2 * pair + 1 - k], lc[pair], 1 - k) + split_dot(
                pot_mid, lt[n], 1
            )
            out_low[n] = out[n].astype(bf16)


def side_potentials(signal, own, got, lt, lc, mc):
    vmem = pl.BlockSpec(memory_space=pltpu.VMEM)
    return pl.pallas_call(
        side_kernel,
        out_shape=(
            jax.ShapeDtypeStruct((4, 64, 256), f32),
            jax.ShapeDtypeStruct((4, 64, 256), bf16),
        ),
        in_specs=[pl.BlockSpec(memory_space=pl.ANY)] + [vmem] * 5,
        out_specs=(vmem,) * 2,
        scratch_shapes=[pltpu.VMEM((4, 64, 256), f32)],
        compiler_params=pltpu.CompilerParams(vmem_limit_bytes=16 << 20),
        cost_estimate=pl.CostEstimate(flops=1 << 24, bytes_accessed=1 << 12, transcendentals=0),
    )(signal, own, got, lt, lc, mc)


def final_kernel(
    half,
    own,
    other,
    side_own,
    side_other,
    mt,
    lt,
    basis,
    near,
    out,
    pot,
    side,
    buf,
    sems,
):
    mine = pl.ds(pl.multiple_of(half[0] * 64, 64), 64)
    rest = pl.ds(pl.multiple_of(64 - half[0] * 64, 64), 64)
    pot[mine, :] = own[...]
    pot[rest, :] = other[...]
    for n in range(4):
        side[n, mine, :] = side_own[n]
        side[n, rest, :] = side_other[n].astype(f32)
    copies = []
    for pair in range(2):
        mid = split_dot(pot[...], mt[pair], 1)
        for k in range(2):
            n = 2 * pair + k
            low = (split_dot(mid, lt[n], 1) + side[n]).astype(bf16)
            far = lax.dot_general(
                basis[n], low, (((1,), (1,)), ((), ())), preferred_element_type=f32
            )
            buf[n] = (near[n] + far).astype(bf16)
            copies.append(pltpu.make_async_copy(buf.at[n], out.at[n], sems.at[n]))
            copies[n].start()
    for copy in copies:
        copy.wait()


def final_product(half, own, other, side_own, side_other, mt, lt, basis, near):
    vmem = pl.BlockSpec(memory_space=pltpu.VMEM)
    return pl.pallas_call(
        final_kernel,
        out_shape=jax.ShapeDtypeStruct((4, 512, 128), bf16),
        in_specs=[pl.BlockSpec(memory_space=pltpu.SMEM)] + [vmem] * 8,
        out_specs=pl.BlockSpec(memory_space=pl.ANY),
        scratch_shapes=[
            pltpu.VMEM((128, 256), f32),
            pltpu.VMEM((4, 128, 256), f32),
            pltpu.VMEM((4, 512, 128), bf16),
            pltpu.SemaphoreType.DMA((4,)),
        ],
        compiler_params=pltpu.CompilerParams(vmem_limit_bytes=16 << 20),
        cost_estimate=pl.CostEstimate(
            flops=2 * 4 * 512 * 256 * 128, bytes_accessed=4 << 20, transcendentals=0
        ),
    )(half, own, other, side_own, side_other, mt, lt, basis, near)


def shards(
    fields,
    near_blocks,
    leaf_basis,
    leaf_transfer,
    mid_transfer,
    leaf_couple,
    mid_couple,
    cross_transfer,
    cross_couple,
):
    place = lax.axis_index("row")
    first_core = (lax.axis_index("leaf") & 1) == 0
    half = ((place ^ (place >> 1)) & 1).reshape(1)
    place = place.reshape(1)

    keep, send, side_keep, side_send = gather_skeletons(
        half, fields, leaf_basis, leaf_transfer, mid_transfer
    )
    basis, lt, mt = leaf_basis, leaf_transfer, mid_transfer
    joint, crown, lc, mc = stage_mats(keep, cross_transfer, cross_couple, leaf_couple, mid_couple)
    with jax.named_scope("row_sum"):
        current = keep + exchange(send, "row", 1)
        (side_send,) = hold(current, side_send)
        got_side = exchange(side_send, "row", 1)
        current = current + exchange(current, "row", 3)

    with jax.named_scope("level0"):
        both = times(current, joint[0])
        lifted = both[:, :256]
        mine = jnp.where(first_core, lifted[:32], lifted[32:])
        other = jnp.where(first_core, lifted[32:], lifted[:32])
        payload = jnp.concatenate([other, both[:, 256:]], axis=0)
        with jax.named_scope("side2"):
            (got_side,) = hold(payload, got_side)
            skel = side_keep + got_side.astype(f32)
            across_side = exchange(skel.astype(bf16), "row", 3)
        got = exchange(payload, "leaf", 1)
        current = mine + got[:32]
        incoming = [got[32:]]

    def prepare(level, current):
        both = times(current, joint[level])
        lifted = both[:, :256]
        payload = jnp.concatenate([*two_terms(lifted), both[:, 256:].astype(bf16)], axis=1)
        return lifted, payload

    def rise(level, lifted, payload):
        got = exchange(payload, "leaf", PARTNERS[level]).astype(f32)
        incoming.append(got[:, 512:])
        return lifted + (got[:, :256] + got[:, 256:512])

    with jax.named_scope("level1"):
        lifted, payload = prepare(1, current)
        with jax.named_scope("ring"):
            ready = after(fields, payload)
            from_left = shifted(ready, 1)
            from_right = shifted(ready, -1)
        current = rise(1, lifted, payload)
    with jax.named_scope("level2"):
        lifted, payload = prepare(2, current)
        across_side, payload = lax.optimization_barrier((across_side, payload))
        with jax.named_scope("near"):
            near = near_product(place, near_blocks, payload, (0,), (fields,))
        with jax.named_scope("side"):
            side, side_send = side_potentials(payload, skel, across_side, lt, lc, mc)
        with jax.named_scope("path"):
            (steps,) = hold(payload, joint[1:5, :, :256])
            path = steps[0].astype(f32)
            for level in (1, 2, 3):
                path = times(path, steps[level])
        current = rise(2, lifted, payload)
    with jax.named_scope("level3"):
        lifted, payload = prepare(3, current)
        near, side, path, payload = lax.optimization_barrier((near, side, path, payload))
        with jax.named_scope("side3"):
            (side_send,) = hold(payload, side_send, flops=1 << 32)
            side_other = exchange(side_send, "row", 1)
        current = rise(3, lifted, payload)
    with jax.named_scope("level4"):
        lifted, payload = prepare(4, current)
        from_left, from_right, side_send, payload = lax.optimization_barrier(
            (from_left, from_right, side_send, payload)
        )
        with jax.named_scope("across"):
            from_left, from_right = hold(payload, from_left, from_right)
            across0 = shifted(from_left[:2], 1)
            across1 = shifted(from_right[2:], -1)
        current = rise(4, lifted, payload)
    with jax.named_scope("level5"):
        payload = times(current, crown).astype(bf16)
        side_other, payload = lax.optimization_barrier((side_other, payload))
        (tail,) = hold(payload, incoming[4])
        for level in (3, 2, 1):
            tail = times_t(tail, joint[level, :, :256]) + incoming[level]
        potential = exchange(payload, "leaf", PARTNERS[5]).astype(f32)

    with jax.named_scope("down"):
        tail, potential = lax.optimization_barrier((tail, potential))
        potential = times_t(potential, path) + tail
        (side,) = hold(potential, side, flops=1 << 32)
        other = exchange(potential, "leaf", 1)
        top = jnp.where(first_core, potential, other)
        bottom = jnp.where(first_core, other, potential)
        potential = times_t(jnp.concatenate([top, bottom]), joint[0, :, :256]) + incoming[0]
        across0, across1, side, potential = lax.optimization_barrier(
            (across0, across1, side, potential)
        )
        with jax.named_scope("near"):
            near = near_product(
                place, near_blocks, potential, (3, 1), (from_left, from_right), near
            )
            near = near_product(place, near_blocks, potential, (2,), (across0, across1), near)
        other = exchange(potential, "row", 1)
    with jax.named_scope("final"):
        return final_product(
            half, potential, other, side, side_other, mt, lt, basis, near
        )


def solution(mesh):
    return jax.shard_map(
        shards,
        mesh=mesh,
        in_specs=(
            P("leaf", "row", None),
            P("leaf", "row", None),
            P("leaf", "row", None),
            P("leaf", None, None),
            P("leaf", None, None),
            P("leaf", None, None),
            P("leaf", None, None),
            P("leaf", None, None, None),
            P("leaf", None, None, None),
        ),
        out_specs=P("leaf", "row", None),
        check_vma=False,
    )
```

```python
import functools

import jax
import jax.numpy as jnp
from jax import lax
from jax.experimental import pallas as pl
from jax.experimental.pallas import tpu as pltpu
from jax.sharding import PartitionSpec as P

bf16 = jnp.bfloat16
f32 = jnp.float32
precise = lax.Precision.HIGHEST
PARTNERS = (1, 2, 4, 12, 16, 48)


def exchange(value, axis, mask):
    count = lax.axis_size(axis)
    return lax.ppermute(value, axis, [(i, i ^ mask) for i in range(count)])


def shifted(value, step):
    count = lax.axis_size("row")
    return lax.ppermute(value, "row", [(i, (i + step) % count) for i in range(count)])


def times(values, mats):
    return lax.dot_general(
        values, mats.astype(f32), (((1,), (0,)), ((), ())), precision=precise
    )


def times_t(values, mats):
    return lax.dot_general(
        values, mats.astype(f32), (((1,), (1,)), ((), ())), precision=precise
    )


def split_dot(values, mats, contract):
    rows = values.shape[0]
    high = values.astype(bf16)
    low = (values - high.astype(f32)).astype(bf16)
    both = lax.dot_general(
        jnp.concatenate([high, low], axis=0),
        mats,
        (((1,), (contract,)), ((), ())),
        preferred_element_type=f32,
    )
    return both[:rows] + both[rows:]


def after(value, *others):
    return lax.optimization_barrier((value,) + others)[0]


def hold(signal, *values, flops=1 << 24):
    anywhere = pl.BlockSpec(memory_space=pl.ANY)
    return pl.pallas_call(
        lambda *refs: None,
        out_shape=tuple(jax.ShapeDtypeStruct(v.shape, v.dtype) for v in values),
        in_specs=[anywhere] * (1 + len(values)),
        out_specs=(anywhere,) * len(values),
        input_output_aliases={1 + i: i for i in range(len(values))},
        compiler_params=pltpu.CompilerParams(vmem_limit_bytes=16 << 20),
        cost_estimate=pl.CostEstimate(flops=flops, bytes_accessed=0, transcendentals=0),
    )(signal, *values)


def two_terms(values):
    high = lax.reduce_precision(values, 8, 7)
    return high.astype(bf16), (values - high).astype(bf16)


def gather_kernel(
    half,
    fields,
    basis,
    lt,
    mt,
    keep,
    send,
    side_keep,
    side_send,
    f_buf,
    basis_out,
    lt_out,
    mt_out,
    scratch,
    sems,
):
    f_copy = pltpu.make_async_copy(fields, f_buf, sems.at[0])
    b_copies = [
        pltpu.make_async_copy(
            basis.at[pl.ds(2 * pair, 2)], basis_out.at[pl.ds(2 * pair, 2)], sems.at[1 + pair]
        )
        for pair in range(2)
    ]
    lt_copy = pltpu.make_async_copy(lt, lt_out, sems.at[3])
    mt_copy = pltpu.make_async_copy(mt, mt_out, sems.at[4])
    for copy in (f_copy, *b_copies, lt_copy, mt_copy):
        copy.start()
    mine = pl.ds(pl.multiple_of(half[0] * 64, 64), 64)
    other = pl.ds(pl.multiple_of(64 - half[0] * 64, 64), 64)
    f_copy.wait()
    for n in range(4):
        if n % 2 == 0:
            b_copies[n // 2].wait()
        scratch[n] = lax.dot_general(
            f_buf[n], basis_out[n], (((0,), (0,)), ((), ())), preferred_element_type=f32
        )
    lt_copy.wait()
    mt_copy.wait()
    current = None
    for pair in range(2):
        mid = split_dot(scratch[2 * pair], lt_out[2 * pair], 0) + split_dot(
            scratch[2 * pair + 1], lt_out[2 * pair + 1], 0
        )
        lifted = split_dot(mid, mt_out[pair], 0)
        current = lifted if current is None else current + lifted
    scratch[4] = current
    keep[...] = scratch[4, mine, :]
    send[...] = scratch[4, other, :]
    for n in range(4):
        side_keep[n] = scratch[n, mine, :]
        side_send[n] = scratch[n, other, :].astype(bf16)


def gather_skeletons(half, fields, basis, lt, mt):
    vmem = pl.BlockSpec(memory_space=pltpu.VMEM)
    return pl.pallas_call(
        gather_kernel,
        out_shape=(
            jax.ShapeDtypeStruct((64, 256), f32),
            jax.ShapeDtypeStruct((64, 256), f32),
            jax.ShapeDtypeStruct((4, 64, 256), f32),
            jax.ShapeDtypeStruct((4, 64, 256), bf16),
        ),
        in_specs=[pl.BlockSpec(memory_space=pltpu.SMEM)] + [pl.BlockSpec(memory_space=pl.ANY)] * 4,
        out_specs=(vmem,) * 4,
        scratch_shapes=[
            pltpu.VMEM((4, 512, 128), bf16),
            pltpu.VMEM((4, 512, 256), bf16),
            pltpu.VMEM((4, 256, 256), bf16),
            pltpu.VMEM((2, 256, 256), bf16),
            pltpu.VMEM((5, 128, 256), f32),
            pltpu.SemaphoreType.DMA((5,)),
        ],
        compiler_params=pltpu.CompilerParams(vmem_limit_bytes=54528 << 10),
        cost_estimate=pl.CostEstimate(
            flops=2 * 4 * 512 * 256 * 128, bytes_accessed=3 << 20, transcendentals=0
        ),
    )(half, fields, basis, lt, mt)


def stage_kernel(keep, ct, cc, joint, sems):
    copies = [
        pltpu.make_async_copy(
            ct.at[0], joint.at[pl.ds(0, 5), :, pl.ds(0, 256)], sems.at[0]
        ),
        pltpu.make_async_copy(cc.at[0], joint.at[:, :, pl.ds(256, 256)], sems.at[1]),
    ]
    for copy in copies:
        copy.start()
    for copy in copies:
        copy.wait()


def stage_mats(keep, ct, cc):
    return pl.pallas_call(
        stage_kernel,
        out_shape=jax.ShapeDtypeStruct((6, 256, 512), bf16),
        in_specs=[pl.BlockSpec(memory_space=pl.ANY)] * 3,
        out_specs=pl.BlockSpec(memory_space=pltpu.VMEM),
        scratch_shapes=[pltpu.SemaphoreType.DMA((2,))],
        compiler_params=pltpu.CompilerParams(vmem_limit_bytes=16 << 20),
        cost_estimate=pl.CostEstimate(flops=0, bytes_accessed=4 << 20, transcendentals=0),
    )(keep, ct, cc)


def near_kernel(offsets, pieces, started, place, near, signal, *refs):
    parts, refs = refs[:pieces], refs[pieces:]
    out = refs[-1]
    for n in range(4):
        total = refs[0][n] if started else None
        for i, offset in enumerate(offsets):
            column = pl.multiple_of(lax.rem(place[0] + offset, 4) * 512, 512)
            part = parts[i][n] if len(offsets) == pieces else parts[n // 2][n % 2]
            term = jnp.dot(near[n, :, pl.ds(column, 512)], part, preferred_element_type=f32)
            total = term if total is None else total + term
        out[n] = total


def near_product(place, near, signal, offsets, parts, so_far=None):
    vmem = pl.BlockSpec(memory_space=pltpu.VMEM)
    extra = () if so_far is None else (so_far,)
    return pl.pallas_call(
        functools.partial(near_kernel, offsets, len(parts), bool(extra)),
        out_shape=jax.ShapeDtypeStruct((4, 512, 128), f32),
        in_specs=[pl.BlockSpec(memory_space=pltpu.SMEM), vmem, pl.BlockSpec(memory_space=pl.ANY)]
        + [vmem] * (len(parts) + len(extra)),
        out_specs=vmem,
        compiler_params=pltpu.CompilerParams(vmem_limit_bytes=24 << 20),
        cost_estimate=pl.CostEstimate(
            flops=1 << 31, bytes_accessed=1 << 12, transcendentals=0
        ),
    )(place, near, signal, *parts, *extra)


def side_kernel(signal, own, got, lt, lc, mc, out, out_low, skel):
    for n in range(4):
        skel[n] = own[n] + got[n].astype(f32)
    mid = [
        split_dot(skel[2 * pair], lt[2 * pair], 0)
        + split_dot(skel[2 * pair + 1], lt[2 * pair + 1], 0)
        for pair in range(2)
    ]
    for pair in range(2):
        pot_mid = split_dot(mid[1 - pair], mc[0], 1 - pair)
        for k in range(2):
            n = 2 * pair + k
            out[n] = split_dot(skel[2 * pair + 1 - k], lc[pair], 1 - k) + split_dot(
                pot_mid, lt[n], 1
            )
            out_low[n] = out[n].astype(bf16)


def side_potentials(signal, own, got, lt, lc, mc):
    vmem = pl.BlockSpec(memory_space=pltpu.VMEM)
    return pl.pallas_call(
        side_kernel,
        out_shape=(
            jax.ShapeDtypeStruct((4, 64, 256), f32),
            jax.ShapeDtypeStruct((4, 64, 256), bf16),
        ),
        in_specs=[pl.BlockSpec(memory_space=pl.ANY)] + [vmem] * 5,
        out_specs=(vmem,) * 2,
        scratch_shapes=[pltpu.VMEM((4, 64, 256), f32)],
        compiler_params=pltpu.CompilerParams(vmem_limit_bytes=16 << 20),
        cost_estimate=pl.CostEstimate(flops=1 << 24, bytes_accessed=1 << 12, transcendentals=0),
    )(signal, own, got, lt, lc, mc)


def final_kernel(
    half,
    own,
    other,
    side_own,
    side_other,
    mt,
    lt,
    basis,
    near,
    out,
    pot,
    side,
    buf,
    sems,
):
    mine = pl.ds(pl.multiple_of(half[0] * 64, 64), 64)
    rest = pl.ds(pl.multiple_of(64 - half[0] * 64, 64), 64)
    pot[mine, :] = own[...]
    pot[rest, :] = other[...]
    for n in range(4):
        side[n, mine, :] = side_own[n]
        side[n, rest, :] = side_other[n].astype(f32)
    copies = []
    for pair in range(2):
        mid = split_dot(pot[...], mt[pair], 1)
        for k in range(2):
            n = 2 * pair + k
            low = (split_dot(mid, lt[n], 1) + side[n]).astype(bf16)
            far = lax.dot_general(
                basis[n], low, (((1,), (1,)), ((), ())), preferred_element_type=f32
            )
            buf[n] = (near[n] + far).astype(bf16)
            copies.append(pltpu.make_async_copy(buf.at[n], out.at[n], sems.at[n]))
            copies[n].start()
    for copy in copies:
        copy.wait()


def final_product(half, own, other, side_own, side_other, mt, lt, basis, near):
    vmem = pl.BlockSpec(memory_space=pltpu.VMEM)
    return pl.pallas_call(
        final_kernel,
        out_shape=jax.ShapeDtypeStruct((4, 512, 128), bf16),
        in_specs=[pl.BlockSpec(memory_space=pltpu.SMEM)] + [vmem] * 8,
        out_specs=pl.BlockSpec(memory_space=pl.ANY),
        scratch_shapes=[
            pltpu.VMEM((128, 256), f32),
            pltpu.VMEM((4, 128, 256), f32),
            pltpu.VMEM((4, 512, 128), bf16),
            pltpu.SemaphoreType.DMA((4,)),
        ],
        compiler_params=pltpu.CompilerParams(vmem_limit_bytes=16 << 20),
        cost_estimate=pl.CostEstimate(
            flops=2 * 4 * 512 * 256 * 128, bytes_accessed=4 << 20, transcendentals=0
        ),
    )(half, own, other, side_own, side_other, mt, lt, basis, near)


def shards(
    fields,
    near_blocks,
    leaf_basis,
    leaf_transfer,
    mid_transfer,
    leaf_couple,
    mid_couple,
    cross_transfer,
    cross_couple,
):
    place = lax.axis_index("row")
    first_core = (lax.axis_index("leaf") & 1) == 0
    half = ((place ^ (place >> 1)) & 1).reshape(1)
    place = place.reshape(1)

    keep, send, side_keep, side_send = gather_skeletons(
        half, fields, leaf_basis, leaf_transfer, mid_transfer
    )
    basis, lt, mt = leaf_basis, leaf_transfer, mid_transfer
    joint = stage_mats(keep, cross_transfer, cross_couple)
    crown = joint[5, :, 256:]
    with jax.named_scope("path"):
        path = joint[1, :, :256].astype(f32)
        for level in (2, 3, 4):
            path = times(path, joint[level, :, :256])
    with jax.named_scope("row_sum"):
        current = keep + exchange(send, "row", 1)
        path, current = lax.optimization_barrier((path, current))
        (side_send,) = hold(current, side_send)
        got_side = exchange(side_send, "row", 1)
        with jax.named_scope("ring0"):
            from_left = shifted(after(fields, side_send), 1)
        current = current + exchange(current, "row", 3)

    with jax.named_scope("level0"):
        both = times(current, joint[0])
        lifted = both[:, :256]
        mine = jnp.where(first_core, lifted[:32], lifted[32:])
        other = jnp.where(first_core, lifted[32:], lifted[:32])
        payload = jnp.concatenate([other, both[:, 256:]], axis=0)
        (mine,) = hold(payload, mine, flops=1 << 32)
        got = exchange(payload, "leaf", 1)
        current = mine + got[:32]
        incoming = [got[32:]]

    def prepare(level, current):
        both = times(current, joint[level])
        lifted = both[:, :256]
        terms = two_terms(lifted)
        payload = jnp.concatenate([*terms, both[:, 256:].astype(bf16)], axis=1)
        return lifted, payload

    def rise(level, lifted, payload):
        got = exchange(payload, "leaf", PARTNERS[level]).astype(f32)
        incoming.append(got[:, -256:])
        partner = got[:, :256]
        if got.shape[1] > 512:
            partner = partner + got[:, 256:512]
        return lifted + partner

    with jax.named_scope("level1"):
        lifted, payload = prepare(1, current)
        with jax.named_scope("side2"):
            (got_side,) = hold(payload, got_side)
            skel = side_keep + got_side.astype(f32)
            side_send = skel.astype(bf16)
            across_side = exchange(side_send, "row", 3)
        with jax.named_scope("ring1"):
            from_right = shifted(after(fields, payload, side_send), -1)
        current = rise(1, lifted, payload)
    with jax.named_scope("level2"):
        lifted, payload = prepare(2, current)
        with jax.named_scope("near"):
            near = near_product(place, near_blocks, payload, (0,), (fields,))
        current = rise(2, lifted, payload)
    with jax.named_scope("level3"):
        lifted, payload = prepare(3, current)
        near, path, payload = lax.optimization_barrier((near, path, payload))
        with jax.named_scope("side3"):
            (across_side,) = hold(payload, across_side, flops=1 << 32)
            side, side_send = side_potentials(payload, skel, across_side, lt, leaf_couple, mid_couple)
            side_other = exchange(side_send, "row", 1)
        current = rise(3, lifted, payload)
    with jax.named_scope("level4"):
        lifted, payload = prepare(4, current)
        side, side_send, payload = lax.optimization_barrier((side, side_send, payload))
        from_left, payload = lax.optimization_barrier((from_left, payload))
        (side,) = hold(payload, side, flops=1 << 32)
        with jax.named_scope("across"):
            (from_left,) = hold(payload, from_left)
            across0 = shifted(from_left[:2], 1)
            (from_right,) = hold(payload, from_right)
            across1 = shifted(from_right[2:], -1)
        current = rise(4, lifted, payload)
    with jax.named_scope("level5"):
        payload = times(current, crown).astype(bf16)
        side_other, side, from_right, payload = lax.optimization_barrier(
            (side_other, side, from_right, payload)
        )
        (tail,) = hold(payload, incoming[4])
        for level in (3, 2, 1):
            tail = times_t(tail, joint[level, :, :256]) + incoming[level]
        potential = exchange(payload, "leaf", PARTNERS[5]).astype(f32)

    with jax.named_scope("down"):
        tail, potential = lax.optimization_barrier((tail, potential))
        potential = times_t(potential, path) + tail
        (side,) = hold(potential, side, flops=1 << 32)
        other = exchange(potential, "leaf", 1)
        top = jnp.where(first_core, potential, other)
        bottom = jnp.where(first_core, other, potential)
        potential = times_t(jnp.concatenate([top, bottom]), joint[0, :, :256]) + incoming[0]
        side, potential = lax.optimization_barrier((side, potential))
        with jax.named_scope("near"):
            near = near_product(
                place, near_blocks, potential, (3, 1), (from_left, from_right), near
            )
            near = near_product(place, near_blocks, potential, (2,), (across0, across1), near)
        other = exchange(potential, "row", 1)
    with jax.named_scope("final"):
        return final_product(
            half, potential, other, side, side_other, mt, lt, basis, near
        )


def solution(mesh):
    return jax.shard_map(
        shards,
        mesh=mesh,
        in_specs=(
            P("leaf", "row", None),
            P("leaf", "row", None),
            P("leaf", "row", None),
            P("leaf", None, None),
            P("leaf", None, None),
            P("leaf", None, None),
            P("leaf", None, None),
            P("leaf", None, None, None),
            P("leaf", None, None, None),
        ),
        out_specs=P("leaf", "row", None),
        check_vma=False,
    )
```

```python
import functools

import jax
import jax.numpy as jnp
from jax import lax
from jax.experimental import pallas as pl
from jax.experimental.pallas import tpu as pltpu
from jax.sharding import PartitionSpec as P

bf16 = jnp.bfloat16
f32 = jnp.float32
precise = lax.Precision.HIGHEST
PARTNERS = (1, 2, 4, 12, 16, 48)


def exchange(value, axis, mask):
    count = lax.axis_size(axis)
    return lax.ppermute(value, axis, [(i, i ^ mask) for i in range(count)])


def shifted(value, step):
    count = lax.axis_size("row")
    return lax.ppermute(value, "row", [(i, (i + step) % count) for i in range(count)])


def times(values, mats):
    return lax.dot_general(
        values, mats.astype(f32), (((1,), (0,)), ((), ())), precision=precise
    )


def times_t(values, mats):
    return lax.dot_general(
        values, mats.astype(f32), (((1,), (1,)), ((), ())), precision=precise
    )


def split_dot(values, mats, contract):
    rows = values.shape[0]
    high = values.astype(bf16)
    low = (values - high.astype(f32)).astype(bf16)
    both = lax.dot_general(
        jnp.concatenate([high, low], axis=0),
        mats,
        (((1,), (contract,)), ((), ())),
        preferred_element_type=f32,
    )
    return both[:rows] + both[rows:]


def after(value, *others):
    return lax.optimization_barrier((value,) + others)[0]


def hold(signal, *values, flops=1 << 24):
    anywhere = pl.BlockSpec(memory_space=pl.ANY)
    return pl.pallas_call(
        lambda *refs: None,
        out_shape=tuple(jax.ShapeDtypeStruct(v.shape, v.dtype) for v in values),
        in_specs=[anywhere] * (1 + len(values)),
        out_specs=(anywhere,) * len(values),
        input_output_aliases={1 + i: i for i in range(len(values))},
        compiler_params=pltpu.CompilerParams(vmem_limit_bytes=16 << 20),
        cost_estimate=pl.CostEstimate(flops=flops, bytes_accessed=0, transcendentals=0),
    )(signal, *values)


def two_terms(values):
    high = lax.reduce_precision(values, 8, 7)
    return high.astype(bf16), (values - high).astype(bf16)


def gather_kernel(
    half,
    fields,
    basis,
    lt,
    mt,
    keep,
    send,
    side_keep,
    side_send,
    f_buf,
    basis_out,
    lt_out,
    mt_out,
    scratch,
    sems,
):
    f_copy = pltpu.make_async_copy(fields, f_buf, sems.at[0])
    lt_copy = pltpu.make_async_copy(lt, lt_out, sems.at[1])
    mt_copy = pltpu.make_async_copy(mt, mt_out, sems.at[2])
    b_copies = [
        pltpu.make_async_copy(basis.at[n], basis_out.at[n], sems.at[3 + n]) for n in range(4)
    ]
    for copy in (f_copy, b_copies[0], lt_copy, *b_copies[1:3], mt_copy, b_copies[3]):
        copy.start()
    mine = pl.ds(pl.multiple_of(half[0] * 64, 64), 64)
    other = pl.ds(pl.multiple_of(64 - half[0] * 64, 64), 64)
    f_copy.wait()
    current = None
    mid = None
    for n in range(4):
        b_copies[n].wait()
        skel = lax.dot_general(
            f_buf[n], basis_out[n], (((0,), (0,)), ((), ())), preferred_element_type=f32
        )
        scratch[n] = skel
        if n == 0:
            lt_copy.wait()
        lifted = split_dot(skel, lt_out[n], 0)
        mid = lifted if n % 2 == 0 else mid + lifted
        if n == 1:
            mt_copy.wait()
        if n % 2:
            lifted = split_dot(mid, mt_out[n // 2], 0)
            current = lifted if current is None else current + lifted
    scratch[4] = current
    keep[...] = scratch[4, mine, :]
    send[...] = scratch[4, other, :]
    for n in range(4):
        side_keep[n] = scratch[n, mine, :]
        side_send[n] = scratch[n, other, :].astype(bf16)


def gather_skeletons(half, fields, basis, lt, mt):
    vmem = pl.BlockSpec(memory_space=pltpu.VMEM)
    return pl.pallas_call(
        gather_kernel,
        out_shape=(
            jax.ShapeDtypeStruct((64, 256), f32),
            jax.ShapeDtypeStruct((64, 256), f32),
            jax.ShapeDtypeStruct((4, 64, 256), f32),
            jax.ShapeDtypeStruct((4, 64, 256), bf16),
        ),
        in_specs=[pl.BlockSpec(memory_space=pltpu.SMEM)] + [pl.BlockSpec(memory_space=pl.ANY)] * 4,
        out_specs=(vmem,) * 4,
        scratch_shapes=[
            pltpu.VMEM((4, 512, 128), bf16),
            pltpu.VMEM((4, 512, 256), bf16),
            pltpu.VMEM((4, 256, 256), bf16),
            pltpu.VMEM((2, 256, 256), bf16),
            pltpu.VMEM((5, 128, 256), f32),
            pltpu.SemaphoreType.DMA((7,)),
        ],
        compiler_params=pltpu.CompilerParams(vmem_limit_bytes=54528 << 10),
        cost_estimate=pl.CostEstimate(
            flops=2 * 4 * 512 * 256 * 128, bytes_accessed=3 << 20, transcendentals=0
        ),
    )(half, fields, basis, lt, mt)


def stage_kernel(keep, ct, cc, joint, sems):
    copies = [
        pltpu.make_async_copy(
            ct.at[0], joint.at[pl.ds(0, 5), :, pl.ds(0, 256)], sems.at[0]
        ),
        pltpu.make_async_copy(cc.at[0], joint.at[:, :, pl.ds(256, 256)], sems.at[1]),
    ]
    for copy in copies:
        copy.start()
    for copy in copies:
        copy.wait()


def stage_mats(keep, ct, cc):
    return pl.pallas_call(
        stage_kernel,
        out_shape=jax.ShapeDtypeStruct((6, 256, 512), bf16),
        in_specs=[pl.BlockSpec(memory_space=pl.ANY)] * 3,
        out_specs=pl.BlockSpec(memory_space=pltpu.VMEM),
        scratch_shapes=[pltpu.SemaphoreType.DMA((2,))],
        compiler_params=pltpu.CompilerParams(vmem_limit_bytes=16 << 20),
        cost_estimate=pl.CostEstimate(flops=0, bytes_accessed=4 << 20, transcendentals=0),
    )(keep, ct, cc)


def near_kernel(offsets, pieces, started, place, near, signal, *refs):
    parts, refs = refs[:pieces], refs[pieces:]
    out = refs[-1]
    for n in range(4):
        total = refs[0][n] if started else None
        for i, offset in enumerate(offsets):
            column = pl.multiple_of(lax.rem(place[0] + offset, 4) * 512, 512)
            part = parts[i][n] if len(offsets) == pieces else parts[n // 2][n % 2]
            term = jnp.dot(near[n, :, pl.ds(column, 512)], part, preferred_element_type=f32)
            total = term if total is None else total + term
        out[n] = total


def near_product(place, near, signal, offsets, parts, so_far=None):
    vmem = pl.BlockSpec(memory_space=pltpu.VMEM)
    extra = () if so_far is None else (so_far,)
    return pl.pallas_call(
        functools.partial(near_kernel, offsets, len(parts), bool(extra)),
        out_shape=jax.ShapeDtypeStruct((4, 512, 128), f32),
        in_specs=[pl.BlockSpec(memory_space=pltpu.SMEM), vmem, pl.BlockSpec(memory_space=pl.ANY)]
        + [vmem] * (len(parts) + len(extra)),
        out_specs=vmem,
        compiler_params=pltpu.CompilerParams(vmem_limit_bytes=24 << 20),
        cost_estimate=pl.CostEstimate(
            flops=1 << 31, bytes_accessed=1 << 12, transcendentals=0
        ),
    )(place, near, signal, *parts, *extra)


def side_kernel(signal, own, got, lt, lc, mc, out, out_low, skel):
    for n in range(4):
        skel[n] = own[n] + got[n].astype(f32)
    mid = [
        split_dot(skel[2 * pair], lt[2 * pair], 0)
        + split_dot(skel[2 * pair + 1], lt[2 * pair + 1], 0)
        for pair in range(2)
    ]
    for pair in range(2):
        pot_mid = split_dot(mid[1 - pair], mc[0], 1 - pair)
        for k in range(2):
            n = 2 * pair + k
            out[n] = split_dot(skel[2 * pair + 1 - k], lc[pair], 1 - k) + split_dot(
                pot_mid, lt[n], 1
            )
            out_low[n] = out[n].astype(bf16)


def side_potentials(signal, own, got, lt, lc, mc):
    vmem = pl.BlockSpec(memory_space=pltpu.VMEM)
    return pl.pallas_call(
        side_kernel,
        out_shape=(
            jax.ShapeDtypeStruct((4, 64, 256), f32),
            jax.ShapeDtypeStruct((4, 64, 256), bf16),
        ),
        in_specs=[pl.BlockSpec(memory_space=pl.ANY)] + [vmem] * 5,
        out_specs=(vmem,) * 2,
        scratch_shapes=[pltpu.VMEM((4, 64, 256), f32)],
        compiler_params=pltpu.CompilerParams(vmem_limit_bytes=16 << 20),
        cost_estimate=pl.CostEstimate(flops=1 << 24, bytes_accessed=1 << 12, transcendentals=0),
    )(signal, own, got, lt, lc, mc)


def final_kernel(
    half,
    own,
    other,
    side_own,
    side_other,
    mt,
    lt,
    basis,
    near,
    out,
    pot,
    side,
    buf,
    sems,
):
    mine = pl.ds(pl.multiple_of(half[0] * 64, 64), 64)
    rest = pl.ds(pl.multiple_of(64 - half[0] * 64, 64), 64)
    pot[mine, :] = own[...]
    pot[rest, :] = other[...]
    for n in range(4):
        side[n, mine, :] = side_own[n]
        side[n, rest, :] = side_other[n].astype(f32)
    mids = [split_dot(pot[...], mt[pair], 1) for pair in range(2)]
    lows = [(split_dot(mids[n // 2], lt[n], 1) + side[n]).astype(bf16) for n in range(4)]
    copies = []
    for n in range(4):
        far = lax.dot_general(
            basis[n], lows[n], (((1,), (1,)), ((), ())), preferred_element_type=f32
        )
        buf[n] = (near[n] + far).astype(bf16)
        copies.append(pltpu.make_async_copy(buf.at[n], out.at[n], sems.at[n]))
        copies[n].start()
    for copy in copies:
        copy.wait()


def final_product(half, own, other, side_own, side_other, mt, lt, basis, near):
    vmem = pl.BlockSpec(memory_space=pltpu.VMEM)
    return pl.pallas_call(
        final_kernel,
        out_shape=jax.ShapeDtypeStruct((4, 512, 128), bf16),
        in_specs=[pl.BlockSpec(memory_space=pltpu.SMEM)] + [vmem] * 8,
        out_specs=pl.BlockSpec(memory_space=pl.ANY),
        scratch_shapes=[
            pltpu.VMEM((128, 256), f32),
            pltpu.VMEM((4, 128, 256), f32),
            pltpu.VMEM((4, 512, 128), bf16),
            pltpu.SemaphoreType.DMA((4,)),
        ],
        compiler_params=pltpu.CompilerParams(vmem_limit_bytes=16 << 20),
        cost_estimate=pl.CostEstimate(
            flops=2 * 4 * 512 * 256 * 128, bytes_accessed=4 << 20, transcendentals=0
        ),
    )(half, own, other, side_own, side_other, mt, lt, basis, near)


def shards(
    fields,
    near_blocks,
    leaf_basis,
    leaf_transfer,
    mid_transfer,
    leaf_couple,
    mid_couple,
    cross_transfer,
    cross_couple,
):
    place = lax.axis_index("row")
    first_core = (lax.axis_index("leaf") & 1) == 0
    half = ((place ^ (place >> 1)) & 1).reshape(1)
    place = place.reshape(1)

    keep, send, side_keep, side_send = gather_skeletons(
        half, fields, leaf_basis, leaf_transfer, mid_transfer
    )
    basis, lt, mt = leaf_basis, leaf_transfer, mid_transfer
    joint = stage_mats(keep, cross_transfer, cross_couple)
    crown = joint[5, :, 256:]
    with jax.named_scope("path"):
        path = joint[1, :, :256].astype(f32)
        for level in (2, 3, 4):
            path = times(path, joint[level, :, :256])
    with jax.named_scope("row_sum"):
        current = keep + exchange(send, "row", 1)
        path, current = lax.optimization_barrier((path, current))
        (side_send,) = hold(current, side_send)
        got_side = exchange(side_send, "row", 1)
        with jax.named_scope("ring0"):
            from_left = shifted(after(fields, side_send), 1)
        current = current + exchange(current, "row", 3)

    with jax.named_scope("level0"):
        both = times(current, joint[0])
        lifted = both[:, :256]
        mine = jnp.where(first_core, lifted[:32], lifted[32:])
        other = jnp.where(first_core, lifted[32:], lifted[:32])
        payload = jnp.concatenate([other, both[:, 256:]], axis=0)
        (mine,) = hold(payload, mine, flops=1 << 32)
        got = exchange(payload, "leaf", 1)
        current = mine + got[:32]
        incoming = [got[32:]]

    def prepare(level, current):
        both = times(current, joint[level])
        lifted = both[:, :256]
        terms = two_terms(lifted)[: 1 if level in (4,) else 2]
        payload = jnp.concatenate([*terms, both[:, 256:].astype(bf16)], axis=1)
        return lifted, payload

    def rise(level, lifted, payload):
        got = exchange(payload, "leaf", PARTNERS[level]).astype(f32)
        incoming.append(got[:, -256:])
        partner = got[:, :256]
        if got.shape[1] > 512:
            partner = partner + got[:, 256:512]
        return lifted + partner

    with jax.named_scope("level1"):
        lifted, payload = prepare(1, current)
        with jax.named_scope("side2"):
            (got_side,) = hold(payload, got_side)
            skel = side_keep + got_side.astype(f32)
            side_send = skel.astype(bf16)
            across_side = exchange(side_send, "row", 3)
        with jax.named_scope("ring1"):
            from_right = shifted(after(fields, payload, side_send), -1)
        current = rise(1, lifted, payload)
    with jax.named_scope("level2"):
        lifted, payload = prepare(2, current)
        with jax.named_scope("near"):
            near = near_product(place, near_blocks, payload, (0,), (fields,))
        current = rise(2, lifted, payload)
    with jax.named_scope("level3"):
        lifted, payload = prepare(3, current)
        near, path, payload = lax.optimization_barrier((near, path, payload))
        with jax.named_scope("side3"):
            (across_side,) = hold(payload, across_side, flops=1 << 32)
            side, side_send = side_potentials(payload, skel, across_side, lt, leaf_couple, mid_couple)
            side_other = exchange(side_send, "row", 1)
        current = rise(3, lifted, payload)
    with jax.named_scope("level4"):
        lifted, payload = prepare(4, current)
        side, side_send, payload = lax.optimization_barrier((side, side_send, payload))
        from_left, payload = lax.optimization_barrier((from_left, payload))
        (side,) = hold(payload, side, flops=1 << 32)
        with jax.named_scope("across"):
            (from_left,) = hold(payload, from_left)
            across0 = shifted(from_left[:2], 1)
            (from_right,) = hold(payload, from_right)
            across1 = shifted(from_right[2:], -1)
        current = rise(4, lifted, payload)
    with jax.named_scope("level5"):
        payload = times(current, crown).astype(bf16)
        side_other, side, from_right, payload = lax.optimization_barrier(
            (side_other, side, from_right, payload)
        )
        (tail,) = hold(payload, incoming[4])
        for level in (3, 2, 1):
            tail = times_t(tail, joint[level, :, :256]) + incoming[level]
        potential = exchange(payload, "leaf", PARTNERS[5]).astype(f32)

    with jax.named_scope("down"):
        tail, potential = lax.optimization_barrier((tail, potential))
        potential = times_t(potential, path) + tail
        (side,) = hold(potential, side, flops=1 << 32)
        other = exchange(potential, "leaf", 1)
        top = jnp.where(first_core, potential, other)
        bottom = jnp.where(first_core, other, potential)
        potential = times_t(jnp.concatenate([top, bottom]), joint[0, :, :256]) + incoming[0]
        side, potential = lax.optimization_barrier((side, potential))
        with jax.named_scope("near"):
            near = near_product(
                place, near_blocks, potential, (3, 1), (from_left, from_right), near
            )
            near = near_product(place, near_blocks, potential, (2,), (across0, across1), near)
        other = exchange(potential, "row", 1)
    with jax.named_scope("final"):
        return final_product(
            half, potential, other, side, side_other, mt, lt, basis, near
        )


def solution(mesh):
    return jax.shard_map(
        shards,
        mesh=mesh,
        in_specs=(
            P("leaf", "row", None),
            P("leaf", "row", None),
            P("leaf", "row", None),
            P("leaf", None, None),
            P("leaf", None, None),
            P("leaf", None, None),
            P("leaf", None, None),
            P("leaf", None, None, None),
            P("leaf", None, None, None),
        ),
        out_specs=P("leaf", "row", None),
        check_vma=False,
    )
```

```python
import functools

import jax
import jax.numpy as jnp
from jax import lax
from jax.experimental import pallas as pl
from jax.experimental.pallas import tpu as pltpu
from jax.sharding import PartitionSpec as P

bf16 = jnp.bfloat16
f32 = jnp.float32
precise = lax.Precision.HIGHEST
PARTNERS = (1, 2, 4, 12, 16, 48)


def exchange(value, axis, mask):
    count = lax.axis_size(axis)
    return lax.ppermute(value, axis, [(i, i ^ mask) for i in range(count)])


def shifted(value, step):
    count = lax.axis_size("row")
    return lax.ppermute(value, "row", [(i, (i + step) % count) for i in range(count)])


def times(values, mats):
    return lax.dot_general(
        values, mats.astype(f32), (((1,), (0,)), ((), ())), precision=precise
    )


def times_t(values, mats):
    return lax.dot_general(
        values, mats.astype(f32), (((1,), (1,)), ((), ())), precision=precise
    )


def split_dot(values, mats, contract):
    rows = values.shape[0]
    high = values.astype(bf16)
    low = (values - high.astype(f32)).astype(bf16)
    both = lax.dot_general(
        jnp.concatenate([high, low], axis=0),
        mats,
        (((1,), (contract,)), ((), ())),
        preferred_element_type=f32,
    )
    return both[:rows] + both[rows:]


def after(value, *others):
    return lax.optimization_barrier((value,) + others)[0]


def hold(signal, *values, flops=1 << 24):
    anywhere = pl.BlockSpec(memory_space=pl.ANY)
    return pl.pallas_call(
        lambda *refs: None,
        out_shape=tuple(jax.ShapeDtypeStruct(v.shape, v.dtype) for v in values),
        in_specs=[anywhere] * (1 + len(values)),
        out_specs=(anywhere,) * len(values),
        input_output_aliases={1 + i: i for i in range(len(values))},
        compiler_params=pltpu.CompilerParams(vmem_limit_bytes=16 << 20),
        cost_estimate=pl.CostEstimate(flops=flops, bytes_accessed=0, transcendentals=0),
    )(signal, *values)


def two_terms(values):
    high = lax.reduce_precision(values, 8, 7)
    return high.astype(bf16), (values - high).astype(bf16)


def gather_kernel(
    half,
    fields,
    basis,
    lt,
    mt,
    keep,
    send,
    side_keep,
    side_send,
    f_buf,
    basis_out,
    lt_out,
    mt_out,
    scratch,
    sems,
):
    f_copy = pltpu.make_async_copy(fields, f_buf, sems.at[0])
    b_copies = [
        pltpu.make_async_copy(
            basis.at[pl.ds(2 * pair, 2)], basis_out.at[pl.ds(2 * pair, 2)], sems.at[1 + pair]
        )
        for pair in range(2)
    ]
    lt_copy = pltpu.make_async_copy(lt, lt_out, sems.at[3])
    mt_copy = pltpu.make_async_copy(mt, mt_out, sems.at[4])
    for copy in (f_copy, *b_copies, lt_copy, mt_copy):
        copy.start()
    mine = pl.ds(pl.multiple_of(half[0] * 64, 64), 64)
    other = pl.ds(pl.multiple_of(64 - half[0] * 64, 64), 64)
    f_copy.wait()
    for n in range(4):
        if n % 2 == 0:
            b_copies[n // 2].wait()
        scratch[n] = lax.dot_general(
            f_buf[n], basis_out[n], (((0,), (0,)), ((), ())), preferred_element_type=f32
        )
    lt_copy.wait()
    mt_copy.wait()
    current = None
    for pair in range(2):
        mid = split_dot(scratch[2 * pair], lt_out[2 * pair], 0) + split_dot(
            scratch[2 * pair + 1], lt_out[2 * pair + 1], 0
        )
        lifted = split_dot(mid, mt_out[pair], 0)
        current = lifted if current is None else current + lifted
    scratch[4] = current
    keep[...] = scratch[4, mine, :]
    send[...] = scratch[4, other, :]
    for n in range(4):
        side_keep[n] = scratch[n, mine, :]
        side_send[n] = scratch[n, other, :].astype(bf16)


def gather_skeletons(half, fields, basis, lt, mt):
    vmem = pl.BlockSpec(memory_space=pltpu.VMEM)
    return pl.pallas_call(
        gather_kernel,
        out_shape=(
            jax.ShapeDtypeStruct((64, 256), f32),
            jax.ShapeDtypeStruct((64, 256), f32),
            jax.ShapeDtypeStruct((4, 64, 256), f32),
            jax.ShapeDtypeStruct((4, 64, 256), bf16),
        ),
        in_specs=[pl.BlockSpec(memory_space=pltpu.SMEM)] + [pl.BlockSpec(memory_space=pl.ANY)] * 4,
        out_specs=(vmem,) * 4,
        scratch_shapes=[
            pltpu.VMEM((4, 512, 128), bf16),
            pltpu.VMEM((4, 512, 256), bf16),
            pltpu.VMEM((4, 256, 256), bf16),
            pltpu.VMEM((2, 256, 256), bf16),
            pltpu.VMEM((5, 128, 256), f32),
            pltpu.SemaphoreType.DMA((5,)),
        ],
        compiler_params=pltpu.CompilerParams(vmem_limit_bytes=54528 << 10),
        cost_estimate=pl.CostEstimate(
            flops=2 * 4 * 512 * 256 * 128, bytes_accessed=3 << 20, transcendentals=0
        ),
    )(half, fields, basis, lt, mt)


def stage_kernel(keep, ct, cc, joint, sems):
    copies = [
        pltpu.make_async_copy(
            ct.at[0], joint.at[pl.ds(0, 5), :, pl.ds(0, 256)], sems.at[0]
        ),
        pltpu.make_async_copy(cc.at[0], joint.at[:, :, pl.ds(256, 256)], sems.at[1]),
    ]
    for copy in copies:
        copy.start()
    for copy in copies:
        copy.wait()


def stage_mats(keep, ct, cc):
    return pl.pallas_call(
        stage_kernel,
        out_shape=jax.ShapeDtypeStruct((6, 256, 512), bf16),
        in_specs=[pl.BlockSpec(memory_space=pl.ANY)] * 3,
        out_specs=pl.BlockSpec(memory_space=pltpu.VMEM),
        scratch_shapes=[pltpu.SemaphoreType.DMA((2,))],
        compiler_params=pltpu.CompilerParams(vmem_limit_bytes=16 << 20),
        cost_estimate=pl.CostEstimate(flops=0, bytes_accessed=4 << 20, transcendentals=0),
    )(keep, ct, cc)


def near_kernel(offsets, pieces, started, place, near, signal, *refs):
    parts, refs = refs[:pieces], refs[pieces:]
    out = refs[-1]
    for n in range(4):
        total = refs[0][n] if started else None
        for i, offset in enumerate(offsets):
            column = pl.multiple_of(lax.rem(place[0] + offset, 4) * 512, 512)
            part = parts[i][n] if len(offsets) == pieces else parts[n // 2][n % 2]
            term = jnp.dot(near[n, :, pl.ds(column, 512)], part, preferred_element_type=f32)
            total = term if total is None else total + term
        out[n] = total


def near_product(place, near, signal, offsets, parts, so_far=None):
    vmem = pl.BlockSpec(memory_space=pltpu.VMEM)
    extra = () if so_far is None else (so_far,)
    return pl.pallas_call(
        functools.partial(near_kernel, offsets, len(parts), bool(extra)),
        out_shape=jax.ShapeDtypeStruct((4, 512, 128), f32),
        in_specs=[pl.BlockSpec(memory_space=pltpu.SMEM), vmem, pl.BlockSpec(memory_space=pl.ANY)]
        + [vmem] * (len(parts) + len(extra)),
        out_specs=vmem,
        compiler_params=pltpu.CompilerParams(vmem_limit_bytes=24 << 20),
        cost_estimate=pl.CostEstimate(
            flops=1 << 31, bytes_accessed=1 << 12, transcendentals=0
        ),
    )(place, near, signal, *parts, *extra)


def side_kernel(signal, own, got, lt, lc, mc, out, out_low, skel):
    for n in range(4):
        skel[n] = own[n] + got[n].astype(f32)
    mid = [
        split_dot(skel[2 * pair], lt[2 * pair], 0)
        + split_dot(skel[2 * pair + 1], lt[2 * pair + 1], 0)
        for pair in range(2)
    ]
    for pair in range(2):
        pot_mid = split_dot(mid[1 - pair], mc[0], 1 - pair)
        for k in range(2):
            n = 2 * pair + k
            out[n] = split_dot(skel[2 * pair + 1 - k], lc[pair], 1 - k) + split_dot(
                pot_mid, lt[n], 1
            )
            out_low[n] = out[n].astype(bf16)


def side_potentials(signal, own, got, lt, lc, mc):
    vmem = pl.BlockSpec(memory_space=pltpu.VMEM)
    return pl.pallas_call(
        side_kernel,
        out_shape=(
            jax.ShapeDtypeStruct((4, 64, 256), f32),
            jax.ShapeDtypeStruct((4, 64, 256), bf16),
        ),
        in_specs=[pl.BlockSpec(memory_space=pl.ANY)] + [vmem] * 5,
        out_specs=(vmem,) * 2,
        scratch_shapes=[pltpu.VMEM((4, 64, 256), f32)],
        compiler_params=pltpu.CompilerParams(vmem_limit_bytes=16 << 20),
        cost_estimate=pl.CostEstimate(flops=1 << 24, bytes_accessed=1 << 12, transcendentals=0),
    )(signal, own, got, lt, lc, mc)


def final_kernel(
    half,
    own,
    other,
    side_own,
    side_other,
    mt,
    lt,
    basis,
    near,
    out,
    pot,
    side,
    buf,
    sems,
):
    mine = pl.ds(pl.multiple_of(half[0] * 64, 64), 64)
    rest = pl.ds(pl.multiple_of(64 - half[0] * 64, 64), 64)
    pot[mine, :] = own[...]
    pot[rest, :] = other[...]
    for n in range(4):
        side[n, mine, :] = side_own[n]
        side[n, rest, :] = side_other[n].astype(f32)
    mids = [split_dot(pot[...], mt[pair], 1) for pair in range(2)]
    lows = [(split_dot(mids[n // 2], lt[n], 1) + side[n]).astype(bf16) for n in range(4)]
    copies = []
    for n in range(4):
        far = lax.dot_general(
            basis[n], lows[n], (((1,), (1,)), ((), ())), preferred_element_type=f32
        )
        buf[n] = (near[n] + far).astype(bf16)
        copies.append(pltpu.make_async_copy(buf.at[n], out.at[n], sems.at[n]))
        copies[n].start()
    for copy in copies:
        copy.wait()


def final_product(half, own, other, side_own, side_other, mt, lt, basis, near):
    vmem = pl.BlockSpec(memory_space=pltpu.VMEM)
    return pl.pallas_call(
        final_kernel,
        out_shape=jax.ShapeDtypeStruct((4, 512, 128), bf16),
        in_specs=[pl.BlockSpec(memory_space=pltpu.SMEM)] + [vmem] * 8,
        out_specs=pl.BlockSpec(memory_space=pl.ANY),
        scratch_shapes=[
            pltpu.VMEM((128, 256), f32),
            pltpu.VMEM((4, 128, 256), f32),
            pltpu.VMEM((4, 512, 128), bf16),
            pltpu.SemaphoreType.DMA((4,)),
        ],
        compiler_params=pltpu.CompilerParams(vmem_limit_bytes=16 << 20),
        cost_estimate=pl.CostEstimate(
            flops=2 * 4 * 512 * 256 * 128, bytes_accessed=4 << 20, transcendentals=0
        ),
    )(half, own, other, side_own, side_other, mt, lt, basis, near)


def shards(
    fields,
    near_blocks,
    leaf_basis,
    leaf_transfer,
    mid_transfer,
    leaf_couple,
    mid_couple,
    cross_transfer,
    cross_couple,
):
    place = lax.axis_index("row")
    first_core = (lax.axis_index("leaf") & 1) == 0
    half = ((place ^ (place >> 1)) & 1).reshape(1)
    place = place.reshape(1)

    keep, send, side_keep, side_send = gather_skeletons(
        half, fields, leaf_basis, leaf_transfer, mid_transfer
    )
    basis, lt, mt = leaf_basis, leaf_transfer, mid_transfer
    joint = stage_mats(keep, cross_transfer, cross_couple)
    crown = joint[5, :, 256:]
    with jax.named_scope("path"):
        path = joint[1, :, :256].astype(f32)
        for level in (2, 3, 4):
            path = times(path, joint[level, :, :256])
    with jax.named_scope("row_sum"):
        current = keep + exchange(send, "row", 1)
        path, current = lax.optimization_barrier((path, current))
        (side_send,) = hold(current, side_send)
        got_side = exchange(side_send, "row", 1)
        with jax.named_scope("ring0"):
            from_left = shifted(after(fields, side_send), 1)
        current = current + exchange(current, "row", 3)

    with jax.named_scope("level0"):
        both = times(current, joint[0])
        lifted = both[:, :256]
        mine = jnp.where(first_core, lifted[:32], lifted[32:])
        other = jnp.where(first_core, lifted[32:], lifted[:32])
        payload = jnp.concatenate([other, both[:, 256:]], axis=0)
        (mine,) = hold(payload, mine, flops=1 << 32)
        got = exchange(payload, "leaf", 1)
        current = mine + got[:32]
        incoming = [got[32:]]

    def prepare(level, current):
        both = times(current, joint[level])
        lifted = both[:, :256]
        terms = two_terms(lifted)[: 1 if level in (4,) else 2]
        payload = jnp.concatenate([*terms, both[:, 256:].astype(bf16)], axis=1)
        return lifted, payload

    def rise(level, lifted, payload):
        got = exchange(payload, "leaf", PARTNERS[level]).astype(f32)
        incoming.append(got[:, -256:])
        partner = got[:, :256]
        if got.shape[1] > 512:
            partner = partner + got[:, 256:512]
        return lifted + partner

    with jax.named_scope("level1"):
        lifted, payload = prepare(1, current)
        with jax.named_scope("side2"):
            (got_side,) = hold(payload, got_side)
            skel = side_keep + got_side.astype(f32)
            side_send = skel.astype(bf16)
            across_side = exchange(side_send, "row", 3)
        with jax.named_scope("ring1"):
            from_right = shifted(after(fields, payload, side_send), -1)
        current = rise(1, lifted, payload)
    with jax.named_scope("level2"):
        lifted, payload = prepare(2, current)
        with jax.named_scope("near"):
            near = near_product(place, near_blocks, payload, (0,), (fields,))
        current = rise(2, lifted, payload)
    with jax.named_scope("level3"):
        lifted, payload = prepare(3, current)
        near, path, payload = lax.optimization_barrier((near, path, payload))
        with jax.named_scope("side3"):
            (across_side,) = hold(payload, across_side, flops=1 << 32)
            side, side_send = side_potentials(payload, skel, across_side, lt, leaf_couple, mid_couple)
            side_other = exchange(side_send, "row", 1)
        current = rise(3, lifted, payload)
    with jax.named_scope("level4"):
        lifted, payload = prepare(4, current)
        side, side_send, payload = lax.optimization_barrier((side, side_send, payload))
        from_left, payload = lax.optimization_barrier((from_left, payload))
        (side,) = hold(payload, side, flops=1 << 32)
        with jax.named_scope("across"):
            (from_left,) = hold(payload, from_left)
            across0 = shifted(from_left[:2], 1)
            (from_right,) = hold(payload, from_right)
            across1 = shifted(from_right[2:], -1)
        current = rise(4, lifted, payload)
    with jax.named_scope("level5"):
        payload = times(current, crown).astype(bf16)
        side_other, side, from_right, payload = lax.optimization_barrier(
            (side_other, side, from_right, payload)
        )
        (tail,) = hold(payload, incoming[4])
        for level in (3, 2, 1):
            tail = times_t(tail, joint[level, :, :256]) + incoming[level]
        potential = exchange(payload, "leaf", PARTNERS[5]).astype(f32)

    with jax.named_scope("down"):
        tail, potential = lax.optimization_barrier((tail, potential))
        potential = times_t(potential, path) + tail
        (side,) = hold(potential, side, flops=1 << 32)
        other = exchange(potential, "leaf", 1)
        top = jnp.where(first_core, potential, other)
        bottom = jnp.where(first_core, other, potential)
        potential = times_t(jnp.concatenate([top, bottom]), joint[0, :, :256]) + incoming[0]
        side, potential = lax.optimization_barrier((side, potential))
        with jax.named_scope("near"):
            near = near_product(
                place, near_blocks, potential, (3, 1), (from_left, from_right), near
            )
            near = near_product(place, near_blocks, potential, (2,), (across0, across1), near)
        other = exchange(potential, "row", 1)
    with jax.named_scope("final"):
        return final_product(
            half, potential, other, side, side_other, mt, lt, basis, near
        )


def solution(mesh):
    return jax.shard_map(
        shards,
        mesh=mesh,
        in_specs=(
            P("leaf", "row", None),
            P("leaf", "row", None),
            P("leaf", "row", None),
            P("leaf", None, None),
            P("leaf", None, None),
            P("leaf", None, None),
            P("leaf", None, None),
            P("leaf", None, None, None),
            P("leaf", None, None, None),
        ),
        out_specs=P("leaf", "row", None),
        check_vma=False,
    )
```
